32 devices in a mesh: brick: 8 (over z, x), scene: 4 (over y, core).
Axes of the slice: x: 2, y: 2, z: 4, core: 2. Of those that a mesh axis runs over, the one named last changes fastest.
Arguments:
- features: float32 [4, 32, 64, 512], P('scene', 'brick'), may hold values from -6 to 6
- cotangent: float32 [4, 32, 64, 512], P('scene', 'brick'), may hold values from -6 to 6
- first_kernel: float32 [27, 64, 64], replicated, may hold values from -0.15625 to 0.15625
- second_kernel: float32 [27, 64, 64], replicated, may hold values from -0.15625 to 0.15625
- counts: int32 [8], P('brick'), may hold values from 1 to 4, as said below
- neighbours: int32 [32, 26], P('brick'), may hold values from -1 to 31, as said below
Outputs:
- out_features: float32 [4, 32, 64, 512], P('scene', 'brick')
- feature_grad: float32 [4, 32, 64, 512], P('scene', 'brick')
- first_grad: float32 [27, 64, 64], replicated
- second_grad: float32 [27, 64, 64], replicated
The draws below stay inside these ranges and needn't reach their ends.
Inputs may be any that keep to these rules, and one draw needn't show every extreme that they name: Index d of brick owns counts[d] bricks in its slots 0 to counts[d] - 1; some index owns 4. `neighbours`: entries name occupied slots; the relation is symmetric (if slot t is the neighbour of s in direction (a, b, c), s is the neighbour of t in (-a, -b, -c)); unoccupied slots have only -1. A neighbour in a direction with c = 0 is owned by the same index of brick, with c = 1 by the same or the next index, with c = -1 by the same or the previous index.
All inputs are finite; a program needn't handle non-finite values.
Results may differ from the reference program's by a relative error of at most 0.0057.
Values may be sent and summed in bfloat16 or wider, within the bound.
A program may use at most 128 MiB of HBM per device.

```python
import jax
import jax.numpy as jnp
from jax import lax

C = 64
E = 8
ZL = 1
V = 512
CAP = 4
SLOTS = 32
SCENES = 4
N_BRICK = 8


offsets = [(a, b, c) for a in (-1, 0, 1) for b in (-1, 0, 1) for c in (-1, 0, 1)]


directions = [item for item in offsets if item != (0, 0, 0)]


def geometry(key):
    base_key = jax.random.fold_in(key, 1234)
    key_level, key_roll = jax.random.split(base_key, 2)
    density = jax.random.randint(key_level, (N_BRICK, 1), 1, 5)
    rolled = jax.random.randint(key_roll, (N_BRICK, CAP), 0, 4)
    chosen = N_BRICK - 1
    row_ids = jnp.arange(N_BRICK, dtype=jnp.int32)[:, None]
    places = jnp.arange(CAP, dtype=jnp.int32)[None, :]
    active = (rolled < density) | (row_ids == chosen) | (places == 0)
    counts = jnp.sum(active.astype(jnp.int32), axis=1)
    scores = jnp.where(active, places, places + CAP)
    slot_order = jnp.argsort(scores, axis=1, stable=True).astype(jnp.int32)
    slot_rank = jnp.argsort(slot_order, axis=1, stable=True).astype(jnp.int32)
    slot_of = jnp.where(active, row_ids * CAP + slot_rank, -1)
    pos_x = slot_order % 2
    pos_y = slot_order // 2 % 2
    pos_z = row_ids * ZL + slot_order // 4
    filled = places < counts[:, None]
    layers = N_BRICK * ZL
    columns = []
    for a, b, c in directions:
        near_x = pos_x + a
        near_y = pos_y + b
        near_z = pos_z + c
        inside = (near_x >= 0) & (near_x < 2) & (near_y >= 0) & (near_y < 2) & (near_z >= 0) & (near_z < layers)
        clipped_z = jnp.clip(near_z, 0, layers - 1)
        owner_row = clipped_z // ZL
        near_place = jnp.clip(near_x, 0, 1) + 2 * jnp.clip(near_y, 0, 1) + 4 * (clipped_z % ZL)
        target = slot_of[owner_row, near_place]
        columns.append(jnp.where(inside & filled, target, -1))
    neighbours = jnp.stack(columns, axis=-1).reshape(N_BRICK * CAP, 26).astype(jnp.int32)
    return (counts.astype(jnp.int32), neighbours)


def draw_counts(key, part):
    return geometry(key)[0]


def draw_neighbours(key, part):
    return geometry(key)[1]


def shard_levels(rng, dims, cuts, smallest, high):
    level = 1.0
    for dim, blocks in cuts:
        heights = jax.random.uniform(jax.random.fold_in(jax.random.fold_in(rng, 6), dim), (blocks,), jnp.float32, smallest / len(cuts), high / len(cuts))
        level = level * jnp.repeat(jnp.exp(heights), dims[dim] // blocks).reshape((-1,) + (1,) * (len(dims) - 1 - dim))
    return level


def centred(key, shape, scale, bound, cuts=(), kind=jnp.bfloat16):
    level = shard_levels(key, shape, cuts, -0.22, 0.18) if cuts else 1.0
    entries = jax.random.normal(key, shape, jnp.float32) * scale * level
    return jnp.minimum(jnp.maximum(entries, -bound), bound).astype(kind)


def setup_inputs(seed: int = 0) -> dict:
    key_list = jax.random.split(jax.random.key(seed), 7)
    features = centred(key_list[0], (SCENES, SLOTS, C, V), 1.0, 6.0, ((0, 4), (1, 8)), jnp.float32)
    cotangent = centred(key_list[1], (SCENES, SLOTS, C, V), 1.0, 6.0, ((0, 4), (1, 8)), jnp.float32)
    first_kernel = centred(key_list[2], (27, C, C), (27 * C) ** -0.5, 0.15625, (), jnp.float32)
    second_kernel = centred(key_list[3], (27, C, C), (27 * C) ** -0.5, 0.15625, (), jnp.float32)
    counts = draw_counts(jax.random.fold_in(key_list[6], 71), 0)
    neighbours = draw_neighbours(jax.random.fold_in(key_list[6], 71), 0)
    return {"features": features, "cotangent": cotangent, "first_kernel": first_kernel, "second_kernel": second_kernel, "counts": counts, "neighbours": neighbours}


offsets = [(a, b, c) for a in (-1, 0, 1) for b in (-1, 0, 1) for c in (-1, 0, 1)]
directions = [item for item in offsets if item != (0, 0, 0)]

def source_range(offset, edge_cells):
    if offset < 0:
        return (edge_cells - 1, edge_cells)
    if offset == 0:
        return (0, edge_cells)
    return (0, 1)

def target_range(offset, edge_cells):
    if offset < 0:
        return (0, 1)
    if offset == 0:
        return (1, edge_cells + 1)
    return (edge_cells + 1, edge_cells + 2)

def assemble(center, sources, indices, present, edge_cells):
    slot_count, chans = (center.shape[0], center.shape[1])
    padded = jnp.zeros((slot_count, chans, edge_cells + 2, edge_cells + 2, edge_cells + 2), center.dtype)
    padded = padded.at[:, :, 1:edge_cells + 1, 1:edge_cells + 1, 1:edge_cells + 1].set(center)
    for number, (a, b, c) in enumerate(directions):
        source = sources[c + 1]
        range_i = source_range(a, edge_cells)
        range_j = source_range(b, edge_cells)
        depth_range = source_range(c, edge_cells) if c == 0 else (0, 1)
        slab_part = source[:, :, range_i[0]:range_i[1], range_j[0]:range_j[1], depth_range[0]:depth_range[1]]
        last_row = source.shape[0] - 1
        chosen_rows = jnp.clip(indices[c + 1][:, number], 0, last_row).astype(jnp.int32)
        picked = jnp.take(slab_part, chosen_rows, axis=0)
        picked = jnp.where(present[:, number][:, None, None, None, None], picked, jnp.zeros_like(picked))
        target_i = target_range(a, edge_cells)
        target_j = target_range(b, edge_cells)
        target_l = target_range(c, edge_cells)
        padded = padded.at[:, :, target_i[0]:target_i[1], target_j[0]:target_j[1], target_l[0]:target_l[1]].set(picked)
    return padded

def window_of(padded, number):
    a, b, c = offsets[number]
    slot_count, chans = (padded.shape[0], padded.shape[1])
    part = padded[:, :, 1 + a:1 + a + E, 1 + b:1 + b + E, 1 + c:1 + c + E]
    return part.reshape(slot_count, chans, E * E * E).astype(jnp.float32)

def apply_kernel(padded, weight, transpose):
    weight_f = weight.astype(jnp.bfloat16).astype(jnp.float32)
    accum = None
    for number in range(27):
        window = window_of(padded, number)
        if transpose:
            term = jnp.einsum('io,sop->sip', weight_f[26 - number], window, precision=lax.Precision.HIGHEST)
        else:
            term = jnp.einsum('io,sip->sop', weight_f[number], window, precision=lax.Precision.HIGHEST)
        accum = term if accum is None else accum + term
    return accum

def kernel_terms(padded, errors):
    errors_f = errors.astype(jnp.bfloat16).astype(jnp.float32)
    return jnp.stack([jnp.einsum('sip,sop->io', window_of(padded, number), errors_f, precision=lax.Precision.HIGHEST) for number in range(27)])

def slope(values):
    sig = jax.nn.sigmoid(values)
    return sig * (1.0 + values * (1.0 - sig))

def reference(features, cotangent, first_kernel, second_kernel, counts, neighbours):
    slot_ids = jnp.arange(SLOTS, dtype=jnp.int32)
    occupied = (slot_ids % CAP < counts[slot_ids // CAP]).astype(jnp.float32)[:, None, None]
    present = neighbours >= 0
    indices = (neighbours, neighbours, neighbours)

    def padded_of(values):
        cubes = values.astype(jnp.bfloat16).reshape(SLOTS, C, E, E, E)
        sources = (cubes[..., E - 1:E], cubes, cubes[..., 0:1])
        return assemble(cubes, sources, indices, present, E)

    def one_scene(pair):
        inputs = pair[0] * occupied
        upstream = pair[1] * occupied
        padded_in = padded_of(inputs)
        first_pre = apply_kernel(padded_in, first_kernel, False)
        hidden = inputs + jax.nn.silu(first_pre)
        padded_hidden = padded_of(hidden)
        second_pre = apply_kernel(padded_hidden, second_kernel, False)
        outputs = hidden + jax.nn.silu(second_pre)
        second_err = upstream * slope(second_pre)
        hidden_grad = upstream + apply_kernel(padded_of(second_err), second_kernel, True)
        second_local = kernel_terms(padded_hidden, second_err)
        first_err = hidden_grad * slope(first_pre)
        input_grad = hidden_grad + apply_kernel(padded_of(first_err), first_kernel, True)
        first_local = kernel_terms(padded_in, first_err)
        return (outputs, input_grad, first_local, second_local)
    outputs, input_grad, first_all, second_all = lax.map(one_scene, (features, cotangent))
    scale = 1.0 / jnp.sqrt(jnp.float32(SCENES * SLOTS * V))
    return (outputs, input_grad, lax.optimization_barrier(jnp.sum(first_all, axis=0)) * scale, lax.optimization_barrier(jnp.sum(second_all, axis=0)) * scale)
```

```python
import functools

import jax
import jax.numpy as jnp
from jax import lax
from jax.experimental import pallas as pl
from jax.experimental.pallas import tpu as pltpu
from jax.sharding import PartitionSpec as P

E = 8
G = E + 2
R = 24
L = 128
MESH = pl.DeviceIdType.MESH
F32, BF16 = jnp.float32, jnp.bfloat16

offsets = [(a, b, c) for a in (-1, 0, 1) for b in (-1, 0, 1) for c in (-1, 0, 1)]
directions = [item for item in offsets if item != (0, 0, 0)]
number_of = {item: n for n, item in enumerate(directions)}


def left(shape):
    return lax.broadcasted_iota(jnp.int32, shape, 1) < L // 2


def swap(v):
    return pltpu.roll(v, L // 2, 1)


def sigmoid(v):
    return 1.0 / (1.0 + jnp.exp(-v))


def kernel(
    nb, S,
    f_ref, g_ref, w1_ref, w2_ref, counts_ref, nbr_ref,
    out_ref, fg_ref, g1_ref, g2_ref,
    pad, x1, x2, x3, w1f, w2f, w1b, w2b, et,
    fin, fup, fpre, fhid, fout, low, high, sbuf, rlow, rhigh,
    send_sem, recv_sem,
):
    C = w1_ref.shape[1]
    me = lax.axis_index("brick")
    rows = E * S * E
    jr = S * E

    barrier = pltpu.get_barrier_semaphore()

    @pl.when(me > 0)
    def _():
        pl.semaphore_signal(barrier, inc=1, device_id={"brick": me - 1}, device_id_type=MESH)

    @pl.when(me < nb - 1)
    def _():
        pl.semaphore_signal(barrier, inc=1, device_id={"brick": me + 1}, device_id_type=MESH)

    def at(s, i, j):
        return ((s * G + i) * G + j) * R

    count = counts_ref[0]
    for s in range(S):
        both = jnp.concatenate([f_ref[0, s], g_ref[0, s]], axis=0).T
        both = jnp.where(s < count, both, 0.0)
        other = swap(both)
        m = left(both.shape)
        f = jnp.where(m, both, other)
        g = jnp.where(m, other, both)
        for i in range(E):
            for j in range(E):
                p = (i * E + j) * E
                fin[i, pl.ds(j * jr + s * E, E), :] = f[p : p + E]
                fup[i, pl.ds(j * jr + s * E, E), :] = g[p : p + E]
                pad[pl.ds(at(s, i + 1, j + 1) + E, E), :] = f[p : p + E]

    low[...] = jnp.zeros_like(low)
    high[...] = jnp.zeros_like(high)

    pl.semaphore_wait(barrier, jnp.where(me > 0, 1, 0) + jnp.where(me < nb - 1, 1, 0))

    def up_copy(n):
        return pltpu.make_async_remote_copy(
            src_ref=sbuf.at[n, 0], dst_ref=rlow.at[n],
            send_sem=send_sem.at[n, 0], recv_sem=recv_sem.at[n, 0],
            device_id={"brick": me + 1}, device_id_type=MESH,
        )

    def down_copy(n):
        return pltpu.make_async_remote_copy(
            src_ref=sbuf.at[n, 1], dst_ref=rhigh.at[n],
            send_sem=send_sem.at[n, 1], recv_sem=recv_sem.at[n, 1],
            device_id={"brick": me - 1}, device_id_type=MESH,
        )

    FR = E * E

    def send(n):
        for s in range(S):
            for i in range(E):
                base = at(s, i + 1, 1)
                high[pl.ds(s * FR + i * E, E), :] = pad[pl.ds(base + E, E, stride=R), :]
                low[pl.ds((S + s) * FR + i * E, E), :] = pad[pl.ds(base + 2 * E - 1, E, stride=R), :]
        m = left((FR, L))
        for q in range(S // 2):
            even, odd = 2 * q, 2 * q + 1
            sbuf[n, 0, pl.ds(q * FR, FR), :] = jnp.where(
                m, low[pl.ds((S + even) * FR, FR), :], low[pl.ds((S + odd) * FR, FR), :]
            ).astype(BF16)
            sbuf[n, 1, pl.ds(q * FR, FR), :] = jnp.where(
                m, high[pl.ds(even * FR, FR), :], high[pl.ds(odd * FR, FR), :]
            ).astype(BF16)

        @pl.when(me < nb - 1)
        def _():
            up_copy(n).start()

        @pl.when(me > 0)
        def _():
            down_copy(n).start()

    def matches(s, d, places):
        t = nbr_ref[s, d]
        t = jnp.where(t >= 0, t - me * S, -4 * S)
        return [t == k for k in places]

    def ring():
        def one(s, carry):
            for (a, b, c), d in number_of.items():
                if c != 0:
                    continue
                is_slot = matches(s, d, [k for k in range(S)])
                for i in range(E) if a == 0 else [E - 1 if a < 0 else 0]:
                    for j in range(E) if b == 0 else [E - 1 if b < 0 else 0]:
                        di = i + 1 if a == 0 else (0 if a < 0 else E + 1)
                        dj = j + 1 if b == 0 else (0 if b < 0 else E + 1)
                        v = jnp.zeros((E, L), F32)
                        for k in range(S):
                            v = jnp.where(is_slot[k], pad[pl.ds(at(k, i + 1, j + 1) + E, E), :], v)
                        dst = pl.multiple_of(at(s, di, dj) + E, E)
                        pad[pl.ds(dst, E), :] = v
            return carry

        lax.fori_loop(0, S, one, 0)

    def receive(n):
        m = left((FR, L))

        def unpack(ref, pool, first):
            for q in range(S // 2):
                v = ref[n, pl.ds(q * FR, FR), :].astype(F32)
                w = swap(v)
                pool[pl.ds((first + 2 * q) * FR, FR), :] = jnp.where(m, v, w)
                pool[pl.ds((first + 2 * q + 1) * FR, FR), :] = jnp.where(m, w, v)

        @pl.when(me > 0)
        def _():
            up_copy(n).wait_recv()
            unpack(rlow, low, 0)

        @pl.when(me < nb - 1)
        def _():
            down_copy(n).wait_recv()
            unpack(rhigh, high, S)

    def faces():
        def one(s, carry):
            for (a, b, c), d in number_of.items():
                if c == 0:
                    continue
                pool, row = (low, E - 1) if c < 0 else (high, 2 * E)
                is_slot = matches(s, d, [k - S if c < 0 else k for k in range(2 * S)])

                def pick(rows):
                    v = None
                    for k in range(2 * S):
                        u = pool[rows(k * FR), :]
                        v = jnp.where(is_slot[k], u, jnp.zeros_like(u) if v is None else v)
                    return v

                edge = lambda o: (E - 1, 0) if o < 0 else (0, E + 1)
                if b == 0:
                    for i in range(E) if a == 0 else [edge(a)[0]]:
                        di = i + 1 if a == 0 else edge(a)[1]
                        v = pick(lambda t: pl.ds(t + i * E, E))
                        pad[pl.ds(at(s, di, 1) + row, E, stride=R), :] = v
                elif a == 0:
                    j, dj = edge(b)
                    v = pick(lambda t: pl.ds(t + j, E, stride=E))
                    pad[pl.ds(at(s, 1, dj) + row, E, stride=R * G), :] = v
                else:
                    (i, di), (j, dj) = edge(a), edge(b)
                    v = pick(lambda t: pl.ds(t + i * E + j, 1))
                    pad[pl.ds(at(s, di, dj) + row, 1), :] = v
            return carry

        lax.fori_loop(0, S, one, 0)

    def build(x):
        def one(i, carry):
            m = left((E, L))
            for j in range(G):
                for s in range(0, S, 2):
                    a, b = [], []
                    for k in (s, s + 1):
                        base = pl.multiple_of(at(k, i, j), E)
                        here = pad[pl.ds(base + E, E), :]
                        a.append(jnp.where(m, pad[pl.ds(base + E - 1, E), :], here))
                        b.append(pad[pl.ds(base + E + 1, E), :])
                    r = j * jr + s * E
                    x[i, r : r + 2 * E, :L] = jnp.concatenate(a, axis=0).astype(BF16)
                    x[i, r : r + 2 * E, L:] = jnp.concatenate(b, axis=0).astype(BF16)
            return carry

        lax.fori_loop(0, G, one, 0)

    def put(i, v):
        for s in range(S):
            for j in range(E):
                pad[pl.ds(pl.multiple_of(at(s, i + 1, j + 1) + E, E), E), :] = v[
                    j * jr + s * E : j * jr + (s + 1) * E
                ]

    place = (0, 1, 2, 0)

    def forward_weights(w_ref, w):
        for a in range(3):
            for c in range(3):
                blocks = [w_ref[9 * a + 3 * b + c] for b in place]
                w[pl.ds(a * 4 * C + c * C, C), :] = jnp.concatenate(blocks, axis=1).astype(BF16)
            w[pl.ds(a * 4 * C + 3 * C, C), :] = jnp.zeros((C, 4 * C), BF16)

    def backward_weights(w_ref, w):
        for n, b in enumerate(place):
            for a in range(3):
                blocks = [w_ref[26 - (9 * a + 3 * b + c)] for c in range(3)]
                blocks.append(jnp.zeros((C, C), F32))
                w[pl.ds(n * C, C), pl.ds(a * 4 * C, 4 * C)] = jnp.concatenate(
                    blocks, axis=1
                ).astype(BF16)

    def conv(x, w, back, finish):
        def one(h, carry):
            parts = []
            for u in range(2):
                i = 2 * h + u
                parts.append(jnp.concatenate([x[i], x[i + 1], x[i + 2]], axis=1))
            y = lax.dot_general(
                jnp.concatenate(parts, axis=0), w[...],
                (((1,), (1 if back else 0,)), ((), ())), preferred_element_type=F32,
            )
            m = left((rows, L))
            done = []
            for u in range(2):
                p = y[u * G * jr : (u + 1) * G * jr, :L]
                q = y[u * G * jr : (u + 1) * G * jr, L:]
                p0, p1 = p[:rows], p[jr : jr + rows]
                q0, q2 = q[:rows], q[2 * jr : 2 * jr + rows]
                done.append(
                    jnp.where(m, p0, p1) + jnp.where(m, q2, q0) + swap(jnp.where(m, q2, p1))
                )
            finish(h, done)
            return carry

        lax.fori_loop(0, E // 2, one, 0)

    def put_errors(h, errs):
        parts = []
        z = jnp.zeros((jr, L), F32)
        m = left((G * jr, L))
        for e in errs:
            p0 = jnp.concatenate([e, z, z], axis=0)
            p1 = jnp.concatenate([z, e, z], axis=0)
            p2 = jnp.concatenate([z, z, e], axis=0)
            parts.append(jnp.concatenate([jnp.where(m, p0, p1), p2], axis=1).astype(BF16))
        t = jnp.concatenate(parts, axis=0).T
        et[h] = t

    def kernel_grad(x, g_out):
        for a in range(3):
            acc = jnp.zeros((3 * C, 4 * C), F32)
            for h in range(E // 2):
                xs = jnp.concatenate([x[2 * h + a], x[2 * h + a + 1]], axis=0)
                acc += jnp.dot(et[h, : 3 * C, :], xs, preferred_element_type=F32)
            g_out[a] = acc

    send(0)
    ring()
    forward_weights(w1_ref, w1f)
    forward_weights(w2_ref, w2f)
    receive(0)
    faces()
    build(x1)

    def first(h, ys):
        for u in range(2):
            i = 2 * h + u
            y = ys[u]
            fpre[i] = y
            hid = fin[i] + y * sigmoid(y)
            fhid[i] = hid
            put(i, hid)

    conv(x1, w1f, False, first)

    send(1)
    ring()
    backward_weights(w1_ref, w1b)
    backward_weights(w2_ref, w2b)
    receive(1)
    faces()
    build(x2)

    def second(h, ys):
        errs = []
        for u in range(2):
            i = 2 * h + u
            y = ys[u]
            q = sigmoid(y)
            fout[i] = fhid[i] + y * q
            err = fup[i] * (q * (1.0 + y * (1.0 - q)))
            put(i, err)
            errs.append(err)
        put_errors(h, errs)

    conv(x2, w2f, False, second)

    send(2)
    ring()
    kernel_grad(x2, g2_ref)
    receive(2)
    faces()
    build(x3)

    def third(h, ys):
        errs = []
        for u in range(2):
            i = 2 * h + u
            grad = fup[i] + ys[u]
            fhid[i] = grad
            y = fpre[i]
            q = sigmoid(y)
            err = grad * (q * (1.0 + y * (1.0 - q)))
            put(i, err)
            errs.append(err)
        put_errors(h, errs)

    conv(x3, w2b, True, third)

    send(3)
    ring()
    kernel_grad(x1, g1_ref)
    receive(3)
    faces()
    build(x2)

    def fourth(h, ys):
        both = []
        for u in range(2):
            i = 2 * h + u
            both.append(jnp.where(left((rows, L)), fout[i], fhid[i] + ys[u]))
        for s in range(S):
            v = jnp.concatenate(
                [
                    both[u][j * jr + s * E : j * jr + (s + 1) * E]
                    for u in range(2)
                    for j in range(E)
                ],
                axis=0,
            ).T
            cols = pl.ds(pl.multiple_of(h * 2 * E * E, 2 * E * E), 2 * E * E)
            out_ref[0, s, :, cols] = v[:C]
            fg_ref[0, s, :, cols] = v[C:]

    conv(x2, w1b, True, fourth)

    @pl.when(me < nb - 1)
    def _():
        for n in range(4):
            up_copy(n).wait_send()

    @pl.when(me > 0)
    def _():
        for n in range(4):
            down_copy(n).wait_send()


def body(features, cotangent, first_kernel, second_kernel, counts, neighbours):
    scenes_here, S, C, V = features.shape
    nb = lax.axis_size("brick")
    jr = S * E
    rows = E * jr
    vmem = pl.BlockSpec(memory_space=pltpu.VMEM)
    smem = pl.BlockSpec(memory_space=pltpu.SMEM)
    field = pltpu.VMEM((E, rows, L), F32)
    windows = pltpu.VMEM((G, G * jr, 2 * L), BF16)
    out, fg, g1, g2 = pl.pallas_call(
        functools.partial(kernel, nb, S),
        out_shape=[
            jax.ShapeDtypeStruct(features.shape, F32),
            jax.ShapeDtypeStruct(features.shape, F32),
            jax.ShapeDtypeStruct((3, 3 * C, 4 * C), F32),
            jax.ShapeDtypeStruct((3, 3 * C, 4 * C), F32),
        ],
        in_specs=[vmem] * 4 + [smem] * 2,
        out_specs=[vmem] * 4,
        scratch_shapes=[
            pltpu.VMEM((S * G * G * R, L), F32),
            windows, windows, windows,
            pltpu.VMEM((12 * C, 4 * C), BF16),
            pltpu.VMEM((12 * C, 4 * C), BF16),
            pltpu.VMEM((4 * C, 12 * C), BF16),
            pltpu.VMEM((4 * C, 12 * C), BF16),
            pltpu.VMEM((E // 2, 4 * C, 2 * G * jr), BF16),
            field, field, field, field, field,
            pltpu.VMEM((2 * S * E * E, L), F32),
            pltpu.VMEM((2 * S * E * E, L), F32),
            pltpu.VMEM((4, 2, S // 2 * E * E, L), BF16),
            pltpu.VMEM((4, S // 2 * E * E, L), BF16),
            pltpu.VMEM((4, S // 2 * E * E, L), BF16),
            pltpu.SemaphoreType.DMA((4, 2)),
            pltpu.SemaphoreType.DMA((4, 2)),
        ],
        compiler_params=pltpu.CompilerParams(
            collective_id=0, has_side_effects=True, vmem_limit_bytes=52 * 2**20
        ),
    )(features, cotangent, first_kernel, second_kernel, counts, neighbours)
    g1, g2 = lax.psum((g1[..., : 3 * C], g2[..., : 3 * C]), ("brick", "scene"))
    total = nb * lax.axis_size("scene") * scenes_here * S * V
    scale = 1.0 / jnp.sqrt(jnp.float32(total))

    def whole(g):
        g = g.reshape(3, 3, C, 3, C)
        return jnp.transpose(g, (0, 1, 3, 4, 2)).reshape(27, C, C) * scale

    return out, fg, whole(g1), whole(g2)


def solution(mesh):
    return jax.shard_map(
        body,
        mesh=mesh,
        in_specs=(
            P("scene", "brick", None, None),
            P("scene", "brick", None, None),
            P(),
            P(),
            P("brick"),
            P("brick", None),
        ),
        out_specs=(P("scene", "brick", None, None), P("scene", "brick", None, None), P(), P()),
        check_vma=False,
    )
```

```python
import functools

import jax
import jax.numpy as jnp
from jax import lax
from jax.experimental import pallas as pl
from jax.experimental.pallas import tpu as pltpu
from jax.sharding import PartitionSpec as P

E = 8
G = E + 2
R = 24
L = 128
MESH = pl.DeviceIdType.MESH
F32, BF16 = jnp.float32, jnp.bfloat16

offsets = [(a, b, c) for a in (-1, 0, 1) for b in (-1, 0, 1) for c in (-1, 0, 1)]
directions = [item for item in offsets if item != (0, 0, 0)]
number_of = {item: n for n, item in enumerate(directions)}


def left(shape):
    return lax.broadcasted_iota(jnp.int32, shape, 1) < L // 2


def swap(v):
    return pltpu.roll(v, L // 2, 1)


def sigmoid(v):
    return 1.0 / (1.0 + jnp.exp(-v))


def kernel(
    nb, ns, S, scale,
    f_ref, g_ref, w1_ref, w2_ref, counts_ref, nbr_ref,
    out_ref, fg_ref, g1_ref, g2_ref,
    pad, x1, x2, x3, w1f, w2f, w1b, w2b, et,
    fin, fup, fpre, fhid, fout, low, high, sbuf, rlow, rhigh,
    part, from_scene, mine, from_brick, full,
    send_sem, recv_sem, sum_send, sum_recv,
):
    C = w1_ref.shape[1]
    me = lax.axis_index("brick")
    rows = E * S * E
    jr = S * E

    barrier = pltpu.get_barrier_semaphore()

    sc = lax.axis_index("scene")
    partners = [{"scene": lax.rem(sc + o, ns)} for o in range(1, ns)]
    partners += [{"brick": lax.rem(me + o, nb)} for o in range(1, nb)]
    for partner in partners:
        pl.semaphore_signal(barrier, inc=1, device_id=partner, device_id_type=MESH)

    def at(s, i, j):
        return ((s * G + i) * G + j) * R

    count = counts_ref[0]
    for s in range(S):
        both = jnp.concatenate([f_ref[0, s], g_ref[0, s]], axis=0).T
        both = jnp.where(s < count, both, 0.0)
        other = swap(both)
        m = left(both.shape)
        f = jnp.where(m, both, other)
        g = jnp.where(m, other, both)
        for i in range(E):
            for j in range(E):
                p = (i * E + j) * E
                fin[i, pl.ds(j * jr + s * E, E), :] = f[p : p + E]
                fup[i, pl.ds(j * jr + s * E, E), :] = g[p : p + E]
                pad[pl.ds(at(s, i + 1, j + 1) + E, E), :] = f[p : p + E]

    low[...] = jnp.zeros_like(low)
    high[...] = jnp.zeros_like(high)

    pl.semaphore_wait(barrier, len(partners))

    def up_copy(n):
        return pltpu.make_async_remote_copy(
            src_ref=sbuf.at[n, 0], dst_ref=rlow.at[n],
            send_sem=send_sem.at[n, 0], recv_sem=recv_sem.at[n, 0],
            device_id={"brick": me + 1}, device_id_type=MESH,
        )

    def down_copy(n):
        return pltpu.make_async_remote_copy(
            src_ref=sbuf.at[n, 1], dst_ref=rhigh.at[n],
            send_sem=send_sem.at[n, 1], recv_sem=recv_sem.at[n, 1],
            device_id={"brick": me - 1}, device_id_type=MESH,
        )

    FR = E * E

    def send(n):
        for s in range(S):
            for i in range(E):
                base = at(s, i + 1, 1)
                high[pl.ds(s * FR + i * E, E), :] = pad[pl.ds(base + E, E, stride=R), :]
                low[pl.ds((S + s) * FR + i * E, E), :] = pad[pl.ds(base + 2 * E - 1, E, stride=R), :]
        m = left((FR, L))
        for q in range(S // 2):
            even, odd = 2 * q, 2 * q + 1
            sbuf[n, 0, pl.ds(q * FR, FR), :] = jnp.where(
                m, low[pl.ds((S + even) * FR, FR), :], low[pl.ds((S + odd) * FR, FR), :]
            ).astype(BF16)
            sbuf[n, 1, pl.ds(q * FR, FR), :] = jnp.where(
                m, high[pl.ds(even * FR, FR), :], high[pl.ds(odd * FR, FR), :]
            ).astype(BF16)

        @pl.when(me < nb - 1)
        def _():
            up_copy(n).start()

        @pl.when(me > 0)
        def _():
            down_copy(n).start()

    def matches(s, d, places):
        t = nbr_ref[s, d]
        t = jnp.where(t >= 0, t - me * S, -4 * S)
        return [t == k for k in places]

    def ring():
        def one(s, carry):
            for (a, b, c), d in number_of.items():
                if c != 0:
                    continue
                is_slot = matches(s, d, [k for k in range(S)])
                for i in range(E) if a == 0 else [E - 1 if a < 0 else 0]:
                    for j in range(E) if b == 0 else [E - 1 if b < 0 else 0]:
                        di = i + 1 if a == 0 else (0 if a < 0 else E + 1)
                        dj = j + 1 if b == 0 else (0 if b < 0 else E + 1)
                        v = jnp.zeros((E, L), F32)
                        for k in range(S):
                            v = jnp.where(is_slot[k], pad[pl.ds(at(k, i + 1, j + 1) + E, E), :], v)
                        dst = pl.multiple_of(at(s, di, dj) + E, E)
                        pad[pl.ds(dst, E), :] = v
            return carry

        lax.fori_loop(0, S, one, 0)

    def receive(n):
        m = left((FR, L))

        def unpack(ref, pool, first):
            for q in range(S // 2):
                v = ref[n, pl.ds(q * FR, FR), :].astype(F32)
                w = swap(v)
                pool[pl.ds((first + 2 * q) * FR, FR), :] = jnp.where(m, v, w)
                pool[pl.ds((first + 2 * q + 1) * FR, FR), :] = jnp.where(m, w, v)

        @pl.when(me > 0)
        def _():
            up_copy(n).wait_recv()
            unpack(rlow, low, 0)

        @pl.when(me < nb - 1)
        def _():
            down_copy(n).wait_recv()
            unpack(rhigh, high, S)

    def faces():
        def one(s, carry):
            for (a, b, c), d in number_of.items():
                if c == 0:
                    continue
                pool, row = (low, E - 1) if c < 0 else (high, 2 * E)
                is_slot = matches(s, d, [k - S if c < 0 else k for k in range(2 * S)])

                def pick(rows):
                    v = None
                    for k in range(2 * S):
                        u = pool[rows(k * FR), :]
                        v = jnp.where(is_slot[k], u, jnp.zeros_like(u) if v is None else v)
                    return v

                edge = lambda o: (E - 1, 0) if o < 0 else (0, E + 1)
                if b == 0:
                    for i in range(E) if a == 0 else [edge(a)[0]]:
                        di = i + 1 if a == 0 else edge(a)[1]
                        v = pick(lambda t: pl.ds(t + i * E, E))
                        pad[pl.ds(at(s, di, 1) + row, E, stride=R), :] = v
                elif a == 0:
                    j, dj = edge(b)
                    v = pick(lambda t: pl.ds(t + j, E, stride=E))
                    pad[pl.ds(at(s, 1, dj) + row, E, stride=R * G), :] = v
                else:
                    (i, di), (j, dj) = edge(a), edge(b)
                    v = pick(lambda t: pl.ds(t + i * E + j, 1))
                    pad[pl.ds(at(s, di, dj) + row, 1), :] = v
            return carry

        lax.fori_loop(0, S, one, 0)

    def build(x):
        def one(i, carry):
            m = left((E, L))
            for j in range(G):
                for s in range(0, S, 2):
                    a, b = [], []
                    for k in (s, s + 1):
                        base = pl.multiple_of(at(k, i, j), E)
                        here = pad[pl.ds(base + E, E), :]
                        a.append(jnp.where(m, pad[pl.ds(base + E - 1, E), :], here))
                        b.append(pad[pl.ds(base + E + 1, E), :])
                    r = j * jr + s * E
                    x[i, r : r + 2 * E, :L] = jnp.concatenate(a, axis=0).astype(BF16)
                    x[i, r : r + 2 * E, L:] = jnp.concatenate(b, axis=0).astype(BF16)
            return carry

        lax.fori_loop(0, G, one, 0)

    def put(i, v):
        for s in range(S):
            for j in range(E):
                pad[pl.ds(pl.multiple_of(at(s, i + 1, j + 1) + E, E), E), :] = v[
                    j * jr + s * E : j * jr + (s + 1) * E
                ]

    place = (0, 1, 2, 0)

    def forward_weights(w_ref, w):
        for a in range(3):
            for c in range(3):
                blocks = [w_ref[9 * a + 3 * b + c] for b in place]
                w[pl.ds(a * 4 * C + c * C, C), :] = jnp.concatenate(blocks, axis=1).astype(BF16)
            w[pl.ds(a * 4 * C + 3 * C, C), :] = jnp.zeros((C, 4 * C), BF16)

    def backward_weights(w_ref, w):
        for n, b in enumerate(place):
            for a in range(3):
                blocks = [w_ref[26 - (9 * a + 3 * b + c)] for c in range(3)]
                blocks.append(jnp.zeros((C, C), F32))
                w[pl.ds(n * C, C), pl.ds(a * 4 * C, 4 * C)] = jnp.concatenate(
                    blocks, axis=1
                ).astype(BF16)

    def conv(x, w, back, finish):
        def one(h, carry):
            parts = []
            for u in range(2):
                i = 2 * h + u
                parts.append(jnp.concatenate([x[i], x[i + 1], x[i + 2]], axis=1))
            y = lax.dot_general(
                jnp.concatenate(parts, axis=0), w[...],
                (((1,), (1 if back else 0,)), ((), ())), preferred_element_type=F32,
            )
            m = left((rows, L))
            done = []
            for u in range(2):
                p = y[u * G * jr : (u + 1) * G * jr, :L]
                q = y[u * G * jr : (u + 1) * G * jr, L:]
                p0, p1 = p[:rows], p[jr : jr + rows]
                q0, q2 = q[:rows], q[2 * jr : 2 * jr + rows]
                done.append(
                    jnp.where(m, p0, p1) + jnp.where(m, q2, q0) + swap(jnp.where(m, q2, p1))
                )
            finish(h, done)
            return carry

        lax.fori_loop(0, E // 2, one, 0)

    def put_errors(h, errs):
        parts = []
        z = jnp.zeros((jr, L), F32)
        m = left((G * jr, L))
        for e in errs:
            p0 = jnp.concatenate([e, z, z], axis=0)
            p1 = jnp.concatenate([z, e, z], axis=0)
            p2 = jnp.concatenate([z, z, e], axis=0)
            parts.append(jnp.concatenate([jnp.where(m, p0, p1), p2], axis=1).astype(BF16))
        t = jnp.concatenate(parts, axis=0).T
        et[h] = t

    CR = 3 * C
    total_rows = full.shape[1]
    Q = total_rows // ns
    q = Q // nb

    def kernel_grad(x, n):
        m = left((CR, L))
        last = []
        for a in range(3):
            acc = jnp.zeros((4 * C, 4 * C), F32)
            for h in range(E // 2):
                xs = jnp.concatenate([x[2 * h + a], x[2 * h + a + 1]], axis=0)
                acc += jnp.dot(et[h], xs, preferred_element_type=F32)
            g = acc.T[:CR]
            part[n, pl.ds(a * CR, CR), :] = g[:, :L].astype(BF16)
            last.append(g[:, L:])
        part[n, pl.ds(3 * CR, CR), :] = jnp.where(m, last[0], last[1]).astype(BF16)
        part[n, pl.ds(4 * CR, CR), :] = last[2].astype(BF16)
        rest = total_rows - 5 * CR
        if rest:
            part[n, pl.ds(5 * CR, rest), :] = jnp.zeros((rest, L), BF16)

    def sum_copies(n, step):
        copies = []
        axis, size, here = ("scene", ns, sc) if step in (0, 3) else ("brick", nb, me)
        first_sem = (0, ns - 1, ns + nb - 2, ns + 2 * nb - 3)[step]
        for o in range(1, size):
            to = lax.rem(here + o, size)
            if step == 0:
                src, dst = part.at[n, pl.ds(pl.multiple_of(to * Q, 16), Q)], from_scene.at[n, o - 1]
            elif step == 1:
                src, dst = mine.at[n, pl.ds(pl.multiple_of(to * q, 16), q)], from_brick.at[n, o - 1]
            elif step == 2:
                src = full.at[n, pl.ds(pl.multiple_of(sc * Q + me * q, 16), q)]
                dst = src
            else:
                src = full.at[n, pl.ds(pl.multiple_of(sc * Q, 16), Q)]
                dst = src
            copies.append(
                pltpu.make_async_remote_copy(
                    src_ref=src, dst_ref=dst,
                    send_sem=sum_send.at[n, first_sem + o - 1],
                    recv_sem=sum_recv.at[n, first_sem + o - 1],
                    device_id={axis: to}, device_id_type=MESH,
                )
            )
        return copies

    def sum_start(n, step):
        for copy in sum_copies(n, step):
            copy.start()

    def sum_wait(n, step):
        for copy in sum_copies(n, step):
            copy.wait_recv()

    def sum_next(n, step):
        sum_wait(n, step)
        if step == 0:
            acc = part[n, pl.ds(pl.multiple_of(sc * Q, 16), Q), :].astype(F32)
            for o in range(ns - 1):
                acc += from_scene[n, o].astype(F32)
            mine[n] = acc.astype(BF16)
        elif step == 1:
            acc = mine[n, pl.ds(pl.multiple_of(me * q, 16), q), :].astype(F32)
            for o in range(nb - 1):
                acc += from_brick[n, o].astype(F32)
            full[n, pl.ds(pl.multiple_of(sc * Q + me * q, 16), q), :] = (acc * scale).astype(BF16)
        sum_start(n, step + 1)

    def sum_end(n, ref):
        sum_wait(n, 3)

        def put_blocks(a, b, v):
            for c in range(3):
                ref[9 * a + 3 * b + c] = v[c * C : (c + 1) * C, :C]

        for a in range(3):
            v = full[n, pl.ds(a * CR, CR), :].astype(F32)
            put_blocks(a, 0, v)
            put_blocks(a, 1, swap(v))
        v = full[n, pl.ds(3 * CR, CR), :].astype(F32)
        put_blocks(0, 2, v)
        put_blocks(1, 2, swap(v))
        put_blocks(2, 2, full[n, pl.ds(4 * CR, CR), :].astype(F32))

    send(0)
    ring()
    forward_weights(w1_ref, w1f)
    forward_weights(w2_ref, w2f)
    receive(0)
    faces()
    build(x1)

    def first(h, ys):
        for u in range(2):
            i = 2 * h + u
            y = ys[u]
            fpre[i] = y
            hid = fin[i] + y * sigmoid(y)
            fhid[i] = hid
            put(i, hid)

    conv(x1, w1f, False, first)

    send(1)
    ring()
    backward_weights(w1_ref, w1b)
    backward_weights(w2_ref, w2b)
    receive(1)
    faces()
    build(x2)

    def second(h, ys):
        errs = []
        for u in range(2):
            i = 2 * h + u
            y = ys[u]
            q = sigmoid(y)
            fout[i] = fhid[i] + y * q
            err = fup[i] * (q * (1.0 + y * (1.0 - q)))
            put(i, err)
            errs.append(err)
        put_errors(h, errs)

    conv(x2, w2f, False, second)

    send(2)
    ring()
    kernel_grad(x2, 1)
    sum_start(1, 0)
    receive(2)
    faces()
    build(x3)

    def third(h, ys):
        errs = []
        for u in range(2):
            i = 2 * h + u
            grad = fup[i] + ys[u]
            fhid[i] = grad
            y = fpre[i]
            q = sigmoid(y)
            err = grad * (q * (1.0 + y * (1.0 - q)))
            put(i, err)
            errs.append(err)
        put_errors(h, errs)

    conv(x3, w2b, True, third)

    send(3)
    ring()
    sum_next(1, 0)
    kernel_grad(x1, 0)
    sum_start(0, 0)
    receive(3)
    sum_next(1, 1)
    faces()
    build(x2)

    def fourth(h, ys):
        both = []
        for u in range(2):
            i = 2 * h + u
            both.append(jnp.where(left((rows, L)), fout[i], fhid[i] + ys[u]))
        for s in range(S):
            v = jnp.concatenate(
                [
                    both[u][j * jr + s * E : j * jr + (s + 1) * E]
                    for u in range(2)
                    for j in range(E)
                ],
                axis=0,
            ).T
            cols = pl.ds(pl.multiple_of(h * 2 * E * E, 2 * E * E), 2 * E * E)
            out_ref[0, s, :, cols] = v[:C]
            fg_ref[0, s, :, cols] = v[C:]

    sum_next(0, 0)
    sum_next(1, 2)
    conv(x2, w1b, True, fourth)

    sum_next(0, 1)
    sum_end(1, g2_ref)
    sum_next(0, 2)
    sum_end(0, g1_ref)
    for n in range(2):
        for step in range(4):
            for copy in sum_copies(n, step):
                copy.wait_send()

    @pl.when(me < nb - 1)
    def _():
        for n in range(4):
            up_copy(n).wait_send()

    @pl.when(me > 0)
    def _():
        for n in range(4):
            down_copy(n).wait_send()


def body(features, cotangent, first_kernel, second_kernel, counts, neighbours):
    scenes_here, S, C, V = features.shape
    nb, ns = lax.axis_size("brick"), lax.axis_size("scene")
    total = nb * ns * scenes_here * S * V
    blocks = 16 * nb * ns
    total_rows = -(-15 * C // blocks) * blocks
    jr = S * E
    rows = E * jr
    vmem = pl.BlockSpec(memory_space=pltpu.VMEM)
    smem = pl.BlockSpec(memory_space=pltpu.SMEM)
    field = pltpu.VMEM((E, rows, L), F32)
    windows = pltpu.VMEM((G, G * jr, 2 * L), BF16)
    out, fg, g1, g2 = pl.pallas_call(
        functools.partial(kernel, nb, ns, S, float(total) ** -0.5),
        out_shape=[
            jax.ShapeDtypeStruct(features.shape, F32),
            jax.ShapeDtypeStruct(features.shape, F32),
            jax.ShapeDtypeStruct(first_kernel.shape, F32),
            jax.ShapeDtypeStruct(first_kernel.shape, F32),
        ],
        in_specs=[vmem] * 4 + [smem] * 2,
        out_specs=[vmem] * 4,
        scratch_shapes=[
            pltpu.VMEM((S * G * G * R, L), F32),
            windows, windows, windows,
            pltpu.VMEM((12 * C, 4 * C), BF16),
            pltpu.VMEM((12 * C, 4 * C), BF16),
            pltpu.VMEM((4 * C, 12 * C), BF16),
            pltpu.VMEM((4 * C, 12 * C), BF16),
            pltpu.VMEM((E // 2, 4 * C, 2 * G * jr), BF16),
            field, field, field, field, field,
            pltpu.VMEM((2 * S * E * E, L), F32),
            pltpu.VMEM((2 * S * E * E, L), F32),
            pltpu.VMEM((4, 2, S // 2 * E * E, L), BF16),
            pltpu.VMEM((4, S // 2 * E * E, L), BF16),
            pltpu.VMEM((4, S // 2 * E * E, L), BF16),
            pltpu.VMEM((2, total_rows, L), BF16),
            pltpu.VMEM((2, ns - 1, total_rows // ns, L), BF16),
            pltpu.VMEM((2, total_rows // ns, L), BF16),
            pltpu.VMEM((2, nb - 1, total_rows // ns // nb, L), BF16),
            pltpu.VMEM((2, total_rows, L), BF16),
            pltpu.SemaphoreType.DMA((4, 2)),
            pltpu.SemaphoreType.DMA((4, 2)),
            pltpu.SemaphoreType.DMA((2, 2 * (nb + ns - 2))),
            pltpu.SemaphoreType.DMA((2, 2 * (nb + ns - 2))),
        ],
        compiler_params=pltpu.CompilerParams(
            collective_id=0, has_side_effects=True, vmem_limit_bytes=52 * 2**20
        ),
    )(features, cotangent, first_kernel, second_kernel, counts, neighbours)
    return out, fg, g1, g2


def solution(mesh):
    return jax.shard_map(
        body,
        mesh=mesh,
        in_specs=(
            P("scene", "brick", None, None),
            P("scene", "brick", None, None),
            P(),
            P(),
            P("brick"),
            P("brick", None),
        ),
        out_specs=(P("scene", "brick", None, None), P("scene", "brick", None, None), P(), P()),
        check_vma=False,
    )
```

```python
import functools

import jax
import jax.numpy as jnp
from jax import lax
from jax.experimental import pallas as pl
from jax.experimental.pallas import tpu as pltpu
from jax.sharding import PartitionSpec as P

E = 8
G = E + 2
R = 24
L = 128
MESH = pl.DeviceIdType.MESH
F32, BF16 = jnp.float32, jnp.bfloat16

offsets = [(a, b, c) for a in (-1, 0, 1) for b in (-1, 0, 1) for c in (-1, 0, 1)]
directions = [item for item in offsets if item != (0, 0, 0)]
number_of = {item: n for n, item in enumerate(directions)}


def left(shape):
    return lax.broadcasted_iota(jnp.int32, shape, 1) < L // 2


def swap(v):
    return pltpu.roll(v, L // 2, 1)


def sigmoid(v):
    return 1.0 / (1.0 + jnp.exp(-v))


def kernel(
    nb, ns, S, scale,
    f_ref, g_ref, w1_ref, w2_ref, counts_ref, nbr_ref,
    out_ref, fg_ref, g1_ref, g2_ref,
    pad, x1, x2, x3, w1f, w2f, w1b, w2b, et,
    fin, fup, fpre, fhid, fout, low, high, sbuf, rlow, rhigh,
    part, from_scene, mine, from_brick, full,
    send_sem, recv_sem, sum_send, sum_recv,
):
    C = w1_ref.shape[1]
    me = lax.axis_index("brick")
    rows = E * S * E
    jr = S * E

    barrier = pltpu.get_barrier_semaphore()

    sc = lax.axis_index("scene")
    partners = [{"scene": lax.rem(sc + o, ns)} for o in range(1, ns)]
    partners += [{"brick": lax.rem(me + o, nb)} for o in range(1, nb)]
    for partner in partners:
        pl.semaphore_signal(barrier, inc=1, device_id=partner, device_id_type=MESH)

    def at(s, i, j):
        return ((s * G + i) * G + j) * R

    count = counts_ref[0]
    for s in range(S):
        both = jnp.concatenate([f_ref[0, s], g_ref[0, s]], axis=0).T
        both = jnp.where(s < count, both, 0.0)
        other = swap(both)
        m = left(both.shape)
        f = jnp.where(m, both, other)
        g = jnp.where(m, other, both)
        for i in range(E):
            for j in range(E):
                p = (i * E + j) * E
                fin[i, pl.ds(j * jr + s * E, E), :] = f[p : p + E]
                fup[i, pl.ds(j * jr + s * E, E), :] = g[p : p + E]
                pad[pl.ds(at(s, i + 1, j + 1) + E, E), :] = f[p : p + E]

    low[...] = jnp.zeros_like(low)
    high[...] = jnp.zeros_like(high)

    pl.semaphore_wait(barrier, len(partners))

    def up_copy(n):
        return pltpu.make_async_remote_copy(
            src_ref=sbuf.at[n, 0], dst_ref=rlow.at[n],
            send_sem=send_sem.at[n, 0], recv_sem=recv_sem.at[n, 0],
            device_id={"brick": me + 1}, device_id_type=MESH,
        )

    def down_copy(n):
        return pltpu.make_async_remote_copy(
            src_ref=sbuf.at[n, 1], dst_ref=rhigh.at[n],
            send_sem=send_sem.at[n, 1], recv_sem=recv_sem.at[n, 1],
            device_id={"brick": me - 1}, device_id_type=MESH,
        )

    FR = E * E

    def send(n):
        for s in range(S):
            for i in range(E):
                base = at(s, i + 1, 1)
                high[pl.ds(s * FR + i * E, E), :] = pad[pl.ds(base + E, E, stride=R), :]
                low[pl.ds((S + s) * FR + i * E, E), :] = pad[pl.ds(base + 2 * E - 1, E, stride=R), :]
        m = left((FR, L))
        for q in range(S // 2):
            even, odd = 2 * q, 2 * q + 1
            sbuf[n, 0, pl.ds(q * FR, FR), :] = jnp.where(
                m, low[pl.ds((S + even) * FR, FR), :], low[pl.ds((S + odd) * FR, FR), :]
            ).astype(BF16)
            sbuf[n, 1, pl.ds(q * FR, FR), :] = jnp.where(
                m, high[pl.ds(even * FR, FR), :], high[pl.ds(odd * FR, FR), :]
            ).astype(BF16)

        @pl.when(me < nb - 1)
        def _():
            up_copy(n).start()

        @pl.when(me > 0)
        def _():
            down_copy(n).start()

    def matches(s, d, places):
        t = nbr_ref[s, d]
        t = jnp.where(t >= 0, t - me * S, -4 * S)
        return [t == k for k in places]

    def ring():
        def one(s, carry):
            for (a, b, c), d in number_of.items():
                if c != 0:
                    continue
                is_slot = matches(s, d, [k for k in range(S)])
                for i in range(E) if a == 0 else [E - 1 if a < 0 else 0]:
                    for j in range(E) if b == 0 else [E - 1 if b < 0 else 0]:
                        di = i + 1 if a == 0 else (0 if a < 0 else E + 1)
                        dj = j + 1 if b == 0 else (0 if b < 0 else E + 1)
                        v = jnp.zeros((E, L), F32)
                        for k in range(S):
                            v = jnp.where(is_slot[k], pad[pl.ds(at(k, i + 1, j + 1) + E, E), :], v)
                        dst = pl.multiple_of(at(s, di, dj) + E, E)
                        pad[pl.ds(dst, E), :] = v
            return carry

        lax.fori_loop(0, S, one, 0)

    def receive(n):
        m = left((FR, L))

        def unpack(ref, pool, first):
            for q in range(S // 2):
                v = ref[n, pl.ds(q * FR, FR), :].astype(F32)
                w = swap(v)
                pool[pl.ds((first + 2 * q) * FR, FR), :] = jnp.where(m, v, w)
                pool[pl.ds((first + 2 * q + 1) * FR, FR), :] = jnp.where(m, w, v)

        @pl.when(me > 0)
        def _():
            up_copy(n).wait_recv()
            unpack(rlow, low, 0)

        @pl.when(me < nb - 1)
        def _():
            down_copy(n).wait_recv()
            unpack(rhigh, high, S)

    def faces():
        def one(s, carry):
            for (a, b, c), d in number_of.items():
                if c == 0:
                    continue
                pool, row = (low, E - 1) if c < 0 else (high, 2 * E)
                is_slot = matches(s, d, [k - S if c < 0 else k for k in range(2 * S)])

                def pick(rows):
                    v = None
                    for k in range(2 * S):
                        u = pool[rows(k * FR), :]
                        v = jnp.where(is_slot[k], u, jnp.zeros_like(u) if v is None else v)
                    return v

                edge = lambda o: (E - 1, 0) if o < 0 else (0, E + 1)
                if b == 0:
                    for i in range(E) if a == 0 else [edge(a)[0]]:
                        di = i + 1 if a == 0 else edge(a)[1]
                        v = pick(lambda t: pl.ds(t + i * E, E))
                        pad[pl.ds(at(s, di, 1) + row, E, stride=R), :] = v
                elif a == 0:
                    j, dj = edge(b)
                    v = pick(lambda t: pl.ds(t + j, E, stride=E))
                    pad[pl.ds(at(s, 1, dj) + row, E, stride=R * G), :] = v
                else:
                    (i, di), (j, dj) = edge(a), edge(b)
                    v = pick(lambda t: pl.ds(t + i * E + j, 1))
                    pad[pl.ds(at(s, di, dj) + row, 1), :] = v
            return carry

        lax.fori_loop(0, S, one, 0)

    def build(x):
        def one(i, carry):
            m = left((E, L))
            for j in range(G):
                for s in range(0, S, 2):
                    a, b = [], []
                    for k in (s, s + 1):
                        base = pl.multiple_of(at(k, i, j), E)
                        here = pad[pl.ds(base + E, E), :]
                        a.append(jnp.where(m, pad[pl.ds(base + E - 1, E), :], here))
                        b.append(pad[pl.ds(base + E + 1, E), :])
                    r = j * jr + s * E
                    x[i, r : r + 2 * E, :L] = jnp.concatenate(a, axis=0).astype(BF16)
                    x[i, r : r + 2 * E, L:] = jnp.concatenate(b, axis=0).astype(BF16)
            return carry

        lax.fori_loop(0, G, one, 0)

    def put(i, v):
        for s in range(S):
            for j in range(E):
                pad[pl.ds(pl.multiple_of(at(s, i + 1, j + 1) + E, E), E), :] = v[
                    j * jr + s * E : j * jr + (s + 1) * E
                ]

    place = (0, 1, 2, 0)

    def forward_weights(w_ref, w):
        for a in range(3):
            for c in range(3):
                blocks = [w_ref[9 * a + 3 * b + c] for b in place]
                w[pl.ds(a * 4 * C + c * C, C), :] = jnp.concatenate(blocks, axis=1).astype(BF16)
            w[pl.ds(a * 4 * C + 3 * C, C), :] = jnp.zeros((C, 4 * C), BF16)

    def backward_weights(w_ref, w):
        for n, b in enumerate(place):
            for a in range(3):
                blocks = [w_ref[26 - (9 * a + 3 * b + c)] for c in range(3)]
                blocks.append(jnp.zeros((C, C), F32))
                w[pl.ds(n * C, C), pl.ds(a * 4 * C, 4 * C)] = jnp.concatenate(
                    blocks, axis=1
                ).astype(BF16)

    def conv(x, w, back, finish, first=0, end=E // 2):
        def one(h, carry):
            parts = []
            for u in range(2):
                i = 2 * h + u
                parts.append(jnp.concatenate([x[i], x[i + 1], x[i + 2]], axis=1))
            y = lax.dot_general(
                jnp.concatenate(parts, axis=0), w[...],
                (((1,), (1 if back else 0,)), ((), ())), preferred_element_type=F32,
            )
            m = left((rows, L))
            done = []
            for u in range(2):
                p = y[u * G * jr : (u + 1) * G * jr, :L]
                q = y[u * G * jr : (u + 1) * G * jr, L:]
                p0, p1 = p[:rows], p[jr : jr + rows]
                q0, q2 = q[:rows], q[2 * jr : 2 * jr + rows]
                done.append(
                    jnp.where(m, p0, p1) + jnp.where(m, q2, q0) + swap(jnp.where(m, q2, p1))
                )
            finish(h, done)
            return carry

        lax.fori_loop(first, end, one, 0)

    def put_errors(h, errs):
        parts = []
        z = jnp.zeros((jr, L), F32)
        m = left((G * jr, L))
        for e in errs:
            p0 = jnp.concatenate([e, z, z], axis=0)
            p1 = jnp.concatenate([z, e, z], axis=0)
            p2 = jnp.concatenate([z, z, e], axis=0)
            parts.append(jnp.concatenate([jnp.where(m, p0, p1), p2], axis=1).astype(BF16))
        t = jnp.concatenate(parts, axis=0).T
        et[:, pl.ds(pl.multiple_of(h * 2 * G * jr, L), 2 * G * jr)] = t

    CR = 3 * C
    total_rows = full.shape[1]
    Q = total_rows // ns
    q = Q // nb

    def kernel_grad(x, n):
        m = left((CR, L))
        last = []
        for a in range(3):
            xs = x[a : a + E].reshape(E * G * jr, 4 * C)
            acc = jnp.dot(et[...], xs, preferred_element_type=F32)
            g = acc.T[:CR]
            part[n, pl.ds(a * CR, CR), :] = g[:, :L].astype(BF16)
            last.append(g[:, L:])
        part[n, pl.ds(3 * CR, CR), :] = jnp.where(m, last[0], last[1]).astype(BF16)
        part[n, pl.ds(4 * CR, CR), :] = last[2].astype(BF16)
        rest = total_rows - 5 * CR
        if rest:
            part[n, pl.ds(5 * CR, rest), :] = jnp.zeros((rest, L), BF16)

    def sum_copies(n, step):
        copies = []
        axis, size, here = ("scene", ns, sc) if step in (0, 3) else ("brick", nb, me)
        first_sem = (0, ns - 1, ns + nb - 2, ns + 2 * nb - 3)[step]
        for o in range(1, size):
            to = lax.rem(here + o, size)
            if step == 0:
                src, dst = part.at[n, pl.ds(pl.multiple_of(to * Q, 16), Q)], from_scene.at[n, o - 1]
            elif step == 1:
                src, dst = mine.at[n, pl.ds(pl.multiple_of(to * q, 16), q)], from_brick.at[n, o - 1]
            elif step == 2:
                src = full.at[n, pl.ds(pl.multiple_of(sc * Q + me * q, 16), q)]
                dst = src
            else:
                src = full.at[n, pl.ds(pl.multiple_of(sc * Q, 16), Q)]
                dst = src
            copies.append(
                pltpu.make_async_remote_copy(
                    src_ref=src, dst_ref=dst,
                    send_sem=sum_send.at[n, first_sem + o - 1],
                    recv_sem=sum_recv.at[n, first_sem + o - 1],
                    device_id={axis: to}, device_id_type=MESH,
                )
            )
        return copies

    def sum_start(n, step):
        for copy in sum_copies(n, step):
            copy.start()

    def sum_wait(n, step):
        for copy in sum_copies(n, step):
            copy.wait_recv()

    def sum_next(n, step):
        sum_wait(n, step)
        if step == 0:
            acc = part[n, pl.ds(pl.multiple_of(sc * Q, 16), Q), :].astype(F32)
            for o in range(ns - 1):
                acc += from_scene[n, o].astype(F32)
            mine[n] = acc.astype(BF16)
        elif step == 1:
            acc = mine[n, pl.ds(pl.multiple_of(me * q, 16), q), :].astype(F32)
            for o in range(nb - 1):
                acc += from_brick[n, o].astype(F32)
            full[n, pl.ds(pl.multiple_of(sc * Q + me * q, 16), q), :] = (acc * scale).astype(BF16)
        sum_start(n, step + 1)

    def sum_end(n, ref):
        sum_wait(n, 3)

        def put_blocks(a, b, v):
            for c in range(3):
                ref[9 * a + 3 * b + c] = v[c * C : (c + 1) * C, :C]

        for a in range(3):
            v = full[n, pl.ds(a * CR, CR), :].astype(F32)
            put_blocks(a, 0, v)
            put_blocks(a, 1, swap(v))
        v = full[n, pl.ds(3 * CR, CR), :].astype(F32)
        put_blocks(0, 2, v)
        put_blocks(1, 2, swap(v))
        put_blocks(2, 2, full[n, pl.ds(4 * CR, CR), :].astype(F32))

    send(0)
    ring()
    forward_weights(w1_ref, w1f)
    forward_weights(w2_ref, w2f)
    receive(0)
    faces()
    build(x1)

    def first(h, ys):
        for u in range(2):
            i = 2 * h + u
            y = ys[u]
            fpre[i] = y
            hid = fin[i] + y * sigmoid(y)
            fhid[i] = hid
            put(i, hid)

    conv(x1, w1f, False, first)

    send(1)
    ring()
    backward_weights(w1_ref, w1b)
    backward_weights(w2_ref, w2b)
    receive(1)
    faces()
    build(x2)

    def second(h, ys):
        errs = []
        for u in range(2):
            i = 2 * h + u
            y = ys[u]
            q = sigmoid(y)
            fout[i] = fhid[i] + y * q
            err = fup[i] * (q * (1.0 + y * (1.0 - q)))
            put(i, err)
            errs.append(err)
        put_errors(h, errs)

    conv(x2, w2f, False, second)

    send(2)
    kernel_grad(x2, 1)
    sum_start(1, 0)
    ring()
    receive(2)
    faces()
    build(x3)

    def third(h, ys):
        errs = []
        for u in range(2):
            i = 2 * h + u
            grad = fup[i] + ys[u]
            fhid[i] = grad
            y = fpre[i]
            q = sigmoid(y)
            err = grad * (q * (1.0 + y * (1.0 - q)))
            put(i, err)
            errs.append(err)
        put_errors(h, errs)

    conv(x3, w2b, True, third)

    send(3)
    sum_next(1, 0)
    kernel_grad(x1, 0)
    sum_start(0, 0)
    ring()
    sum_next(1, 1)
    receive(3)
    faces()
    build(x2)
    sum_next(0, 0)
    sum_next(1, 2)

    def fourth(h, ys):
        both = []
        for u in range(2):
            i = 2 * h + u
            both.append(jnp.where(left((rows, L)), fout[i], fhid[i] + ys[u]))
        for s in range(S):
            v = jnp.concatenate(
                [
                    both[u][j * jr + s * E : j * jr + (s + 1) * E]
                    for u in range(2)
                    for j in range(E)
                ],
                axis=0,
            ).T
            cols = pl.ds(pl.multiple_of(h * 2 * E * E, 2 * E * E), 2 * E * E)
            out_ref[0, s, :, cols] = v[:C]
            fg_ref[0, s, :, cols] = v[C:]

    conv(x2, w1b, True, fourth, 0, E // 4)
    sum_next(0, 1)
    conv(x2, w1b, True, fourth, E // 4, E // 2)

    sum_next(0, 2)
    sum_end(1, g2_ref)
    sum_end(0, g1_ref)
    for n in range(2):
        for step in range(4):
            for copy in sum_copies(n, step):
                copy.wait_send()

    @pl.when(me < nb - 1)
    def _():
        for n in range(4):
            up_copy(n).wait_send()

    @pl.when(me > 0)
    def _():
        for n in range(4):
            down_copy(n).wait_send()


def body(features, cotangent, first_kernel, second_kernel, counts, neighbours):
    scenes_here, S, C, V = features.shape
    nb, ns = lax.axis_size("brick"), lax.axis_size("scene")
    total = nb * ns * scenes_here * S * V
    blocks = 16 * nb * ns
    total_rows = -(-15 * C // blocks) * blocks
    jr = S * E
    rows = E * jr
    vmem = pl.BlockSpec(memory_space=pltpu.VMEM)
    smem = pl.BlockSpec(memory_space=pltpu.SMEM)
    field = pltpu.VMEM((E, rows, L), F32)
    windows = pltpu.VMEM((G, G * jr, 2 * L), BF16)
    out, fg, g1, g2 = pl.pallas_call(
        functools.partial(kernel, nb, ns, S, float(total) ** -0.5),
        out_shape=[
            jax.ShapeDtypeStruct(features.shape, F32),
            jax.ShapeDtypeStruct(features.shape, F32),
            jax.ShapeDtypeStruct(first_kernel.shape, F32),
            jax.ShapeDtypeStruct(first_kernel.shape, F32),
        ],
        in_specs=[vmem] * 4 + [smem] * 2,
        out_specs=[vmem] * 4,
        scratch_shapes=[
            pltpu.VMEM((S * G * G * R, L), F32),
            windows, windows, windows,
            pltpu.VMEM((12 * C, 4 * C), BF16),
            pltpu.VMEM((12 * C, 4 * C), BF16),
            pltpu.VMEM((4 * C, 12 * C), BF16),
            pltpu.VMEM((4 * C, 12 * C), BF16),
            pltpu.VMEM((4 * C, E * G * jr), BF16),
            field, field, field, field, field,
            pltpu.VMEM((2 * S * E * E, L), F32),
            pltpu.VMEM((2 * S * E * E, L), F32),
            pltpu.VMEM((4, 2, S // 2 * E * E, L), BF16),
            pltpu.VMEM((4, S // 2 * E * E, L), BF16),
            pltpu.VMEM((4, S // 2 * E * E, L), BF16),
            pltpu.VMEM((2, total_rows, L), BF16),
            pltpu.VMEM((2, ns - 1, total_rows // ns, L), BF16),
            pltpu.VMEM((2, total_rows // ns, L), BF16),
            pltpu.VMEM((2, nb - 1, total_rows // ns // nb, L), BF16),
            pltpu.VMEM((2, total_rows, L), BF16),
            pltpu.SemaphoreType.DMA((4, 2)),
            pltpu.SemaphoreType.DMA((4, 2)),
            pltpu.SemaphoreType.DMA((2, 2 * (nb + ns - 2))),
            pltpu.SemaphoreType.DMA((2, 2 * (nb + ns - 2))),
        ],
        compiler_params=pltpu.CompilerParams(
            collective_id=0, has_side_effects=True, vmem_limit_bytes=52 * 2**20
        ),
    )(features, cotangent, first_kernel, second_kernel, counts, neighbours)
    return out, fg, g1, g2


def solution(mesh):
    return jax.shard_map(
        body,
        mesh=mesh,
        in_specs=(
            P("scene", "brick", None, None),
            P("scene", "brick", None, None),
            P(),
            P(),
            P("brick"),
            P("brick", None),
        ),
        out_specs=(P("scene", "brick", None, None), P("scene", "brick", None, None), P(), P()),
        check_vma=False,
    )
```
